32 devices in a mesh: groups: 2 (over y), ent: 16 (over z, x, core).
Axes of the slice: x: 2, y: 2, z: 4, core: 2. Of those that a mesh axis runs over, the one named last changes fastest.
Arguments:
- counts: int32 [32], P(('groups', 'ent')), parts along dimension 0, may hold values from 1 to 12, 96 in all
- src_index: int32 [384, 256], P(('groups', 'ent')), parts along dimension 0, may hold values from 0 to 1023
- dst_index: int32 [384, 256], P(('groups', 'ent')), parts along dimension 0, may hold values from 0 to 1023
- rel_index: int32 [384, 256], P(('groups', 'ent')), parts along dimension 0, may hold values from 0 to 4095
- neg_index: int32 [384, 512], P(('groups', 'ent')), parts along dimension 0, may hold values from 0 to 1023
- entity_table: bfloat16 [32768, 512], P(('groups', 'ent')), parts along dimension 0, may hold values from -1.1953125 to 1.1953125
- relation_table: float32 [4096, 512], replicated, may hold values from -6 to 6
Outputs:
- grad_table: float32 [32768, 512], P(('groups', 'ent')), parts along dimension 0
- grad_relation: float32 [8192, 512], P(('groups', 'ent')), parts along dimension 0
The draws below stay inside these ranges and needn't reach their ends.
There are 2 independent parts, one for each index of `groups`. The reference program is written for one: setup_inputs(seed, part) draws one part's arguments, and reference() takes and returns one part's arrays. A program takes and returns all parts, laid end to end along the dimension named above; an argument that names none is the same for every part. Nothing has to cross between parts.
Inputs may be any that keep to these rules, and one draw needn't show every extreme that they name: The counts sum to 96, and the largest equals 12.
All inputs are finite; a program needn't handle non-finite values. No bound on the sum of `counts` on one device may be relied on, other than what follows from the above.
Results may differ from the reference program's by a relative error of at most 0.0029.
Values may be sent and summed in bfloat16 or wider, within the bound.
No kernel may reach another device: no remote copies, remote signals or barrier semaphores. Data moves between devices by JAX's collectives and lax.ppermute only.
A program may use at most 64 MiB of HBM per device.

```python
import math
import jax
import jax.numpy as jnp
import numpy as np
from jax import lax

D = 512
NEG = 512
C = 256
CAP = 12
R = 4096
E_DEV = 1024
ENT = 16384
N_ENT = 16


def place_ends(values, stream_key, smallest, high):
    dims = values.shape
    place = [jax.random.randint(jax.random.fold_in(stream_key, axis), (), 0, dims[axis]) for axis in range(len(dims))]
    values = values.at[tuple(place)].set(smallest)
    longest = dims.index(max(dims))
    place[longest] = (place[longest] + 1) % dims[longest]
    return values.at[tuple(place)].set(high)


def shard_levels(own_key, extent, split, low, high):
    factor_of, own = 1.0, jax.random.fold_in(own_key, 6)
    for axis_at, blocks in split:
        steps = jnp.exp(jax.random.uniform(jax.random.fold_in(own, axis_at), (blocks,), jnp.float32, low / len(split), high / len(split)))
        factor_of = factor_of * jnp.repeat(steps, extent[axis_at] // blocks).reshape([-1 if axis == axis_at else 1 for axis in range(len(extent))])
    return factor_of


def rank_table(amount, slope):
    loads = [(1 << 20) // math.isqrt(rank ** slope) + 1 for rank in range(1, amount + 1)]
    scale = 1 + sum(loads) // (1 << 30)
    return np.cumsum(np.array([max(1, weight // scale) for weight in loads]))


def ranked_ids(stream_key, dims, number_of, lean):
    listing = rank_table(number_of, lean)
    lot = jax.random.randint(jax.random.fold_in(stream_key, 1), dims, 0, int(listing[number_of - 1]))
    standing = jnp.searchsorted(jnp.asarray(listing, jnp.int32), lot, side="right")
    return jax.random.permutation(jax.random.fold_in(stream_key, 2), number_of)[standing].astype(jnp.int32)


def profile(count, total, reach, skew):
    weights = [(1 << 20) // math.isqrt(standing ** skew) + 1 for standing in range(2, count + 1)]
    surplus, given = total - reach - (count - 1), [1] * (count - 1)
    while surplus > 0:
        movable = [i for i in range(count - 1) if given[i] < reach]
        mass, left = sum([weights[i] for i in movable]), surplus
        for i in movable:
            more = min(reach - given[i], max(1, left * weights[i] // mass), surplus)
            given[i] = given[i] + more
            surplus = surplus - more
    return np.array([reach] + given)


def uneven_parts(key, amount, total, bound, skew):
    if amount == 2:
        one = jax.random.randint(key, (), max(1, total - bound), min(bound, total - 1) + 1)
        return jnp.stack([one, total - one])
    tallies = jnp.asarray(profile(amount, total, bound, skew), jnp.int32)
    pairs = (amount - 1) // 2
    source_of, receiver = tallies[1:1 + 2 * pairs:2], tallies[2:2 + 2 * pairs:2]
    slack = jnp.minimum(source_of - 1, bound - receiver)
    shifted = jax.random.randint(jax.random.fold_in(key, 1), (pairs,), 0, 1 << 20) % (slack + 1)
    tallies = tallies.at[1:1 + 2 * pairs:2].set(source_of - shifted).at[2:2 + 2 * pairs:2].set(receiver + shifted)
    return tallies[jax.random.permutation(jax.random.fold_in(key, 2), amount)]


def gaussian(key, shape, scale, bound, split=(), kind=jnp.bfloat16):
    result = jax.random.normal(key, shape, jnp.float32) * scale
    if len(split) > 0:
        result = shard_levels(key, shape, split, -0.22, 0.18) * result
    return jnp.clip(result, min=-bound, max=bound).astype(kind)


def setup_inputs(seed: int = 0, part: int = 0) -> dict:
    key_list = jax.random.split(jax.random.key(seed), 8)
    own_keys = jax.random.split(jax.random.fold_in(key_list[7], part), 8)
    return {
        "counts": uneven_parts(own_keys[0], N_ENT, N_ENT * CAP // 2, CAP, 2).astype(jnp.int32),
        "src_index": place_ends(jax.random.randint(own_keys[1], (N_ENT * CAP, C), 0, E_DEV), jax.random.fold_in(own_keys[1], 1), 0, E_DEV - 1).astype(jnp.int32),
        "dst_index": place_ends(jax.random.randint(own_keys[2], (N_ENT * CAP, C), 0, E_DEV), jax.random.fold_in(own_keys[2], 1), 0, E_DEV - 1).astype(jnp.int32),
        "rel_index": place_ends(ranked_ids(own_keys[3], (N_ENT * CAP, C), R, 2), jax.random.fold_in(own_keys[3], 3), 0, R - 1).astype(jnp.int32),
        "neg_index": place_ends(jax.random.randint(own_keys[4], (N_ENT * CAP, NEG), 0, E_DEV), jax.random.fold_in(own_keys[4], 1), 0, E_DEV - 1).astype(jnp.int32),
        "entity_table": gaussian(own_keys[5], (ENT, D), 0.2, 1.1953125, ((0, 16),)),
        "relation_table": gaussian(key_list[6], (R, D), 1.0, 6.0, (), jnp.float32),
    }


margin = 0.1


def rounded(values):
    half = lax.optimization_barrier(values.astype(jnp.bfloat16))
    return half.astype(jnp.float32)


def span_grads(src_rows, dst_rows, neg_rows, rel_rows):
    source = src_rows.astype(jnp.float32)
    target = dst_rows.astype(jnp.float32)
    rotated = source * rel_rows
    positive = jnp.sum(rotated * target, axis=1)
    rotated_half = rotated.astype(jnp.bfloat16)
    negative = jnp.dot(rotated_half, neg_rows.T, preferred_element_type=jnp.float32)
    weights = jax.nn.sigmoid(negative - positive[:, None] + margin)
    totals = jnp.sum(weights, axis=1)
    weights_half = weights.astype(jnp.bfloat16)
    grad_rot = jnp.dot(weights_half, neg_rows, preferred_element_type=jnp.float32) - totals[:, None] * target
    grad_dst = -totals[:, None] * rotated
    grad_neg = jnp.dot(weights_half.T, rotated_half, preferred_element_type=jnp.float32)
    return grad_rot * rel_rows, grad_dst, grad_neg, grad_rot * source


def reference(counts, src_index, dst_index, rel_index, neg_index, entity_table, relation_table):
    parts = counts.shape[0]
    spans = src_index.shape[0]
    slots = spans // parts

    def visit(state, span):
        owner = (span // slots).astype(jnp.int32)
        target_part = ((owner + parts // 2) % parts).astype(jnp.int32)

        def work(pair):
            grad_tab, grad_rel_acc = pair
            src_ids = owner * E_DEV + src_index[span]
            dst_ids = target_part * E_DEV + dst_index[span]
            neg_ids = target_part * E_DEV + neg_index[span]
            rel_ids = rel_index[span]
            grad_src, grad_dst, grad_neg, grad_rel = span_grads(
                entity_table[src_ids], entity_table[dst_ids], entity_table[neg_ids], relation_table[rel_ids])
            grad_tab = grad_tab.at[src_ids].add(rounded(grad_src))
            grad_tab = grad_tab.at[dst_ids].add(rounded(grad_dst))
            grad_tab = grad_tab.at[neg_ids].add(rounded(grad_neg))
            grad_rel_acc = grad_rel_acc + jax.ops.segment_sum(grad_rel, rel_ids, num_segments=R)
            return grad_tab, grad_rel_acc

        def skip_over(pair):
            return pair

        in_use = (span % slots) < counts[owner]
        return lax.cond(in_use, work, skip_over, state), None

    start = (jnp.zeros((ENT, D), jnp.float32), jnp.zeros((R, D), jnp.float32))
    final, _ = lax.scan(visit, start, jnp.arange(spans, dtype=jnp.int32))
    return final[0], final[1]
```

```python
import functools

import jax
import jax.numpy as jnp
from jax import lax
from jax.experimental import pallas as pl
from jax.experimental.pallas import tpu as pltpu
from jax.sharding import PartitionSpec as P

margin = 0.1
BF = jnp.bfloat16
F32 = jnp.float32
BATCH = 16
LANES = 128


def list_row(info_ref, j, cap):
    pos = 2 * j + info_ref[2]
    second = pos >= info_ref[0]
    row = jnp.where(second, cap + pos - info_ref[0], pos)
    return row, second.astype(jnp.int32)


def span_count(info_ref):
    return (info_ref[0] + info_ref[1] + 1 - info_ref[2]) // 2


def pick_column(block, row):
    lane = lax.broadcasted_iota(jnp.int32, block.shape, 1)
    return jnp.sum(jnp.where(lane == row, block, 0), axis=1, keepdims=True)


def prep_kernel(cap, info_ref, rel_ids_ref, neg_t_ref, table_ref, rows_ref, mult_ref):
    edges = rel_ids_ref.shape[1]
    ents = mult_ref.shape[2]

    def span(j, carry):
        row, _ = list_row(info_ref, j, cap)

        def fetch(b, c):
            for i in range(BATCH):
                e = b * BATCH + i
                rows_ref[j, pl.ds(e, 1), :] = table_ref[pl.ds(rel_ids_ref[row, e], 1), :]
            return c

        lax.fori_loop(0, edges // BATCH, fetch, 0)
        total = jnp.zeros((8, ents), F32)
        neg = pick_column(neg_t_ref[...], row)
        lane = lax.broadcasted_iota(jnp.int32, (8, ents), 1)
        for k in range(neg.shape[0] // 8):
            total = total + jnp.where(lane == neg[8 * k : 8 * k + 8], 1.0, 0.0)
        mult_ref[j] = jnp.sum(total, axis=0, keepdims=True)
        return carry

    lax.fori_loop(0, span_count(info_ref), span, 0)


def main_kernel(
    cap, info_ref, rel_ids_ref, ids_t_ref, ids_ref, rel_rows_ref, mult_ref, own_ref, far_ref,
    acc_ref, rel_acc_ref, table, flat,
):
    edges = rel_ids_ref.shape[1]
    ents, width = own_ref.shape
    pieces = width // LANES
    table[0] = own_ref[...]
    table[1] = far_ref[...]
    acc_ref[...] = jnp.zeros(acc_ref.shape, F32)

    def clear(i, c):
        rel_acc_ref[pl.ds(i * 64, 64)] = jnp.zeros((64, pieces, LANES), F32)
        return c

    lax.fori_loop(0, rel_acc_ref.shape[0] // 64, clear, 0)

    def span(j, carry):
        row, way = list_row(info_ref, j, cap)
        src = pick_column(ids_t_ref[0:edges, :], row)
        dst = pick_column(ids_t_ref[edges : 2 * edges, :], row)
        rel = pick_column(ids_t_ref[2 * edges : 3 * edges, :], row)
        src_row = ids_ref[pl.ds(row, 1), 0:edges]
        rel_row = ids_ref[pl.ds(row, 1), 2 * edges : 3 * edges]
        lane = lax.broadcasted_iota(jnp.int32, (edges, ents), 1)
        near_table = table[way]
        far_table = table[1 - way]
        take = jnp.where(lane == src, 1.0, 0.0).astype(BF)
        source = jnp.dot(take, near_table, preferred_element_type=F32)
        rel_rows = rel_rows_ref[j]
        rotated = source * rel_rows
        score = lax.dot_general(
            rotated.astype(BF), far_table, (((1,), (1,)), ((), ())), preferred_element_type=F32
        )
        hit = lane == dst
        positive = jnp.sum(jnp.where(hit, score, 0.0), axis=1, keepdims=True)
        weights = pl.reciprocal(1.0 + jnp.exp(positive - margin - score), approx=True)
        weights = weights * mult_ref[j]
        totals = jnp.sum(weights, axis=1, keepdims=True)
        inverse = 1.0 / jnp.maximum(totals, 1e-30)
        mixed = (weights * inverse - jnp.where(hit, 1.0, 0.0)).astype(BF)
        grad_rot = jnp.dot(mixed, far_table, preferred_element_type=F32) * totals
        acc_ref[1 - way] += lax.dot_general(
            mixed, (rotated * totals).astype(BF), (((0,), (0,)), ((), ())), preferred_element_type=F32
        )
        level = lax.broadcasted_iota(jnp.int32, (ents, edges), 0)
        put = jnp.where(level == src_row, 1.0, 0.0).astype(BF)
        acc_ref[way] += jnp.dot(put, (grad_rot * rel_rows).astype(BF), preferred_element_type=F32)
        e0 = lax.broadcasted_iota(jnp.int32, (edges, edges), 0) // BATCH
        e1 = lax.broadcasted_iota(jnp.int32, (edges, edges), 1) // BATCH
        same = jnp.where((rel == rel_row) & (e0 == e1), 1.0, 0.0).astype(BF)
        summed = jnp.dot(same, (grad_rot * source).astype(BF), preferred_element_type=F32)
        for q in range(pieces):
            flat[:, q, :] = summed[:, q * LANES : (q + 1) * LANES]

        def add_rows(b, c):
            base = b * BATCH
            where_to = [rel_ids_ref[row, base + i] for i in range(BATCH)]
            sums = [rel_acc_ref[where_to[i]] + flat[base + i] for i in range(BATCH)]
            for i in range(BATCH):
                rel_acc_ref[where_to[i]] = sums[i]
            return c

        lax.fori_loop(0, edges // BATCH, add_rows, 0)
        return carry

    lax.fori_loop(0, span_count(info_ref), span, 0)


VMEM = pl.BlockSpec(memory_space=pltpu.VMEM)
SMEM = pl.BlockSpec(memory_space=pltpu.SMEM)


def shards(counts, src_index, dst_index, rel_index, neg_index, entity_table, relation_table):
    devices = lax.axis_size("ent")
    half = devices // 2
    cap, edges = src_index.shape
    negs = neg_index.shape[1]
    ents, width = entity_table.shape
    rels = relation_table.shape[0]
    pieces = width // LANES
    me = lax.axis_index("ent")
    leads = [i for i in range(half) if i % 2 == 0] + [i for i in range(half, devices) if i % 2 == 1]
    lead = (me % 2) == (me // half)

    cross = [((i + half) % devices, i) for i in leads]
    to_mate = [(i, i ^ 1) for i in leads]
    from_mate = [(i ^ 1, i) for i in leads]
    swap = [(i, i ^ 1) for i in range(devices)]

    ids = jnp.concatenate([src_index, dst_index, rel_index, neg_index], axis=1)
    mine = jnp.concatenate([ids, jnp.broadcast_to(counts[0], (8, ids.shape[1]))], axis=0)
    other = lax.ppermute(mine, "ent", cross)
    both = jnp.concatenate([mine, other], axis=0)
    both = jnp.where(lead, both, lax.ppermute(both, "ent", to_mate))
    own = jnp.where(lead, entity_table, lax.ppermute(entity_table, "ent", to_mate))
    far = lax.ppermute(entity_table, "ent", cross)
    far = jnp.where(lead, far, lax.ppermute(far, "ent", to_mate))

    step = cap + 8
    ids = jnp.concatenate([both[:cap], both[step : step + cap]], axis=0)
    info = jnp.stack([both[cap, 0], both[step + cap, 0], jnp.where(lead, 0, 1)]).astype(jnp.int32)
    ids_t = ids.T
    rel_ids = ids[:, 2 * edges : 3 * edges]

    rel_rows, mult = pl.pallas_call(
        functools.partial(prep_kernel, cap),
        out_shape=(
            jax.ShapeDtypeStruct((cap, edges, width), F32),
            jax.ShapeDtypeStruct((cap, 1, ents), F32),
        ),
        in_specs=[SMEM, SMEM, VMEM, VMEM],
        out_specs=(VMEM, VMEM),
        compiler_params=pltpu.CompilerParams(vmem_limit_bytes=24 << 20),
        cost_estimate=pl.CostEstimate(flops=0, bytes_accessed=30 << 20, transcendentals=0),
        name="prep",
    )(info, rel_ids, ids_t[3 * edges :], relation_table)

    acc, rel_acc = pl.pallas_call(
        functools.partial(main_kernel, cap),
        out_shape=(
            jax.ShapeDtypeStruct((2, ents, width), F32),
            jax.ShapeDtypeStruct((rels, pieces, LANES), F32),
        ),
        in_specs=[SMEM, SMEM] + [VMEM] * 6,
        out_specs=(VMEM, VMEM),
        scratch_shapes=[
            pltpu.VMEM((2, ents, width), BF),
            pltpu.VMEM((edges, pieces, LANES), F32),
        ],
        compiler_params=pltpu.CompilerParams(vmem_limit_bytes=48 << 20),
        name="spans",
    )(info, rel_ids, ids_t[: 3 * edges], ids[:, : 3 * edges], rel_rows, mult, own, far)

    part = ents // 2
    far_acc = acc[1]
    low, high = far_acc[:part], far_acc[part:]
    give = jnp.where(lead, high, low).astype(BF)
    keep = jnp.where(lead, low, high)
    far_sum = (keep + lax.ppermute(give, "ent", swap).astype(F32)).astype(BF)
    from_leads = [(i, (i + half) % devices) for i in leads]
    from_mates = [(i ^ 1, (i + half) % devices) for i in leads]
    first = lax.ppermute(far_sum, "ent", from_leads)
    second = lax.ppermute(far_sum, "ent", from_mates)
    near = lax.ppermute(acc[0].astype(BF), "ent", from_mate)
    grad_table = jnp.where(
        lead, acc[0] + near.astype(F32), jnp.concatenate([first, second], axis=0).astype(F32)
    )

    total = rel_acc.reshape(devices, rels // devices, pieces, LANES)
    bit = 1
    while bit < devices:
        total = total.reshape(total.shape[0] // 2, 2, *total.shape[1:])
        mine_bit = (me // bit) % 2
        give = jnp.where(mine_bit == 0, total[:, 1], total[:, 0]).astype(BF)
        keep = jnp.where(mine_bit == 0, total[:, 0], total[:, 1])
        got = lax.ppermute(give, "ent", [(i, i ^ bit) for i in range(devices)])
        total = keep.astype(F32) + got.astype(F32)
        bit *= 2
    grad_relation = total.reshape(rels // devices, width)
    return (grad_table, grad_relation)


def solution(mesh):
    in_specs = (
        P(("groups", "ent")),
        P(("groups", "ent"), None),
        P(("groups", "ent"), None),
        P(("groups", "ent"), None),
        P(("groups", "ent"), None),
        P(("groups", "ent"), None),
        P(),
    )
    out_specs = (P(("groups", "ent"), None), P(("groups", "ent"), None))
    return jax.shard_map(shards, mesh=mesh, in_specs=in_specs, out_specs=out_specs, check_vma=False)
```

```python
import functools

import jax
import jax.numpy as jnp
from jax import lax
from jax.experimental import pallas as pl
from jax.experimental.pallas import tpu as pltpu
from jax.sharding import PartitionSpec as P

margin = 0.1
BF = jnp.bfloat16
F32 = jnp.float32
BATCH = 16
LANES = 128
CHUNKS = 2

VMEM = pl.BlockSpec(memory_space=pltpu.VMEM)
SMEM = pl.BlockSpec(memory_space=pltpu.SMEM)
ANY = pl.BlockSpec(memory_space=pl.ANY)
HBM = pl.BlockSpec(memory_space=pltpu.HBM)


def list_row(info_ref, j, cap):
    pos = 2 * j + info_ref[2]
    second = pos >= info_ref[0]
    row = jnp.where(second, cap + pos - info_ref[0], pos)
    return row, second.astype(jnp.int32)


def span_count(info_ref):
    return (info_ref[0] + info_ref[1] + 1 - info_ref[2]) // 2


def pick_column(block, row):
    lane = lax.broadcasted_iota(jnp.int32, block.shape, 1)
    return jnp.sum(jnp.where(lane == row, block, 0), axis=1, keepdims=True)


def pack_kernel(counts_ref, *refs):
    arrays, out_ref, held, sems = refs[:4], refs[4], refs[5:9], refs[9]
    copies = [pltpu.make_async_copy(arrays[i], held[i], sems.at[i]) for i in range(4)]
    for copy in copies:
        copy.start()
    cap, length = arrays[0].shape[0], out_ref.shape[1]
    out_ref[...] = jnp.full(out_ref.shape, counts_ref[0], jnp.int32)
    at = 0
    for copy, ref in zip(copies, held):
        copy.wait()
        out_ref[:cap, at : at + ref.shape[1]] = ref[...]
        at += ref.shape[1]


def relay_kernel(x_ref, dep_ref, out_ref, sem):
    copy = pltpu.make_async_copy(x_ref, out_ref, sem)
    copy.start()
    copy.wait()


def prep_kernel(cap, info_ref, rel_ids_ref, ids_t_ref, table_ref, rows_ref, mult_ref):
    edges = rel_ids_ref.shape[1]
    ents = mult_ref.shape[2]

    def span(j, carry):
        row, _ = list_row(info_ref, j, cap)
        for e in range(edges):
            rows_ref[j, pl.ds(e, 1), :] = table_ref[pl.ds(rel_ids_ref[row, e], 1), :]
        total = jnp.zeros((8, ents), F32)
        neg = pick_column(ids_t_ref[3 * edges :, :], row)
        lane = lax.broadcasted_iota(jnp.int32, (8, ents), 1)
        for k in range(neg.shape[0] // 8):
            total = total + jnp.where(lane == neg[8 * k : 8 * k + 8], 1.0, 0.0)
        mult_ref[j] = jnp.sum(total, axis=0, keepdims=True)
        return carry

    lax.fori_loop(0, span_count(info_ref), span, 0)


def span_kernel(
    cap, info_ref, rel_ids_ref, ids_t_ref, ids_ref, rel_rows_ref, mult_ref,
    table_ref, far_ref, mate_table_ref, mate_far_ref,
    mixed_ref, scaled_ref, near_ref, *rest,
):
    keep_refs, give_refs = rest[:CHUNKS], rest[CHUNKS : 2 * CHUNKS]
    table, rel_acc, flat, rows, row_sems, table_sems = rest[2 * CHUNKS :]
    edges = rel_ids_ref.shape[1]
    ents = table_ref.shape[0]
    count = span_count(info_ref)

    @pl.when(info_ref[2] == 0)
    def _():
        pltpu.make_async_copy(table_ref, table.at[0], table_sems.at[0]).start()
        pltpu.make_async_copy(far_ref, table.at[1], table_sems.at[1]).start()

    @pl.when(info_ref[2] != 0)
    def _():
        pltpu.make_async_copy(mate_table_ref, table.at[0], table_sems.at[0]).start()
        pltpu.make_async_copy(mate_far_ref, table.at[1], table_sems.at[1]).start()

    def clear(i, c):
        rel_acc[pl.ds(i * 64, 64)] = jnp.zeros((64, *rel_acc.shape[1:]), F32)
        return c

    lax.fori_loop(0, rel_acc.shape[0] // 64, clear, 0)
    flat[...] = jnp.zeros(flat.shape, F32)
    pltpu.make_async_copy(table_ref, table.at[0], table_sems.at[0]).wait()
    pltpu.make_async_copy(far_ref, table.at[1], table_sems.at[1]).wait()

    def add_rows(row):
        for b in range(edges // BATCH):
            where_to = [rel_ids_ref[row, b * BATCH + i] for i in range(BATCH)]
            sums = [rel_acc[where_to[i]] + flat[b * BATCH + i] for i in range(BATCH)]
            for i in range(BATCH):
                rel_acc[where_to[i]] = sums[i]

    def fetch(j):
        slot = lax.rem(j, 2)
        return pltpu.make_async_copy(rel_rows_ref.at[j], rows.at[slot], row_sems.at[slot])

    @pl.when(count > 0)
    def _():
        fetch(0).start()

    e0 = lax.broadcasted_iota(jnp.int32, (edges, edges), 0) // BATCH
    e1 = lax.broadcasted_iota(jnp.int32, (edges, edges), 1) // BATCH

    def span(j, carry):
        fetch(j).wait()

        @pl.when(j + 1 < count)
        def _():
            fetch(j + 1).start()

        add_rows(list_row(info_ref, jnp.maximum(j - 1, 0), cap)[0])
        row, way = list_row(info_ref, j, cap)
        src = pick_column(ids_t_ref[0:edges, :], row)
        dst = pick_column(ids_t_ref[edges : 2 * edges, :], row)
        rel = pick_column(ids_t_ref[2 * edges : 3 * edges, :], row)
        rel_row = ids_ref[pl.ds(row, 1), 2 * edges : 3 * edges]
        lane = lax.broadcasted_iota(jnp.int32, (edges, ents), 1)
        far_table = table[1 - way]
        take = jnp.where(lane == src, 1.0, 0.0).astype(BF)
        source = jnp.dot(take, table[way], preferred_element_type=F32)
        rel_rows = rows[lax.rem(j, 2)]
        rotated = source * rel_rows
        score = lax.dot_general(
            rotated.astype(BF), far_table, (((1,), (1,)), ((), ())), preferred_element_type=F32
        )
        hit = lane == dst
        positive = jnp.sum(jnp.where(hit, score, 0.0), axis=1, keepdims=True)
        weights = mult_ref[j] / (1.0 + jnp.exp(positive - margin - score))
        totals = jnp.sum(weights, axis=1, keepdims=True)
        inverse = 1.0 / jnp.maximum(totals, 1e-30)
        mixed = (weights * inverse - jnp.where(hit, 1.0, 0.0)).astype(BF)
        mixed_ref[j] = mixed
        scaled_ref[j] = (rotated * totals).astype(BF)
        grad_rot = jnp.dot(mixed, far_table, preferred_element_type=F32) * totals
        near_ref[j] = (grad_rot * rel_rows).astype(BF)
        same = jnp.where((rel == rel_row) & (e0 == e1), 1.0, 0.0).astype(BF)
        grad_rel = grad_rot * source
        coarse = grad_rel.astype(BF)
        fine = (grad_rel - coarse.astype(F32)).astype(BF)
        summed = jnp.dot(same, coarse, preferred_element_type=F32) + jnp.dot(
            same, fine, preferred_element_type=F32
        )
        for q in range(flat.shape[1]):
            flat[:, q, :] = summed[:, q * LANES : (q + 1) * LANES]
        return carry

    lax.fori_loop(0, count, span, 0)

    @pl.when(count > 0)
    def _():
        add_rows(list_row(info_ref, jnp.maximum(count - 1, 0), cap)[0])

    pairs, part = keep_refs[0].shape[0], keep_refs[0].shape[1] // flat.shape[1]
    core = info_ref[3]

    def hand_out(c, carry):
        for h in range(CHUNKS):
            mine = (2 * c + core) * CHUNKS * part + h * part
            theirs = (2 * c + 1 - core) * CHUNKS * part + h * part
            keep_refs[h][c] = rel_acc[pl.ds(mine, part)].reshape(keep_refs[h].shape[1:])
            give_refs[h][c] = rel_acc[pl.ds(theirs, part)].reshape(keep_refs[h].shape[1:]).astype(BF)
        return carry

    lax.fori_loop(0, pairs, hand_out, 0)


def table_kernel(cap, side, info_ref, ids_ref, mixed_ref, scaled_ref, near_ref, dep_ref, acc_ref):
    edges, ents = near_ref.shape[1], acc_ref.shape[0]
    acc_ref[...] = jnp.zeros(acc_ref.shape, F32)

    def span(j, carry):
        row, way = list_row(info_ref, j, cap)

        @pl.when(way != side)
        def _():
            acc_ref[...] += lax.dot_general(
                mixed_ref[j], scaled_ref[j], (((0,), (0,)), ((), ())), preferred_element_type=F32
            )

        @pl.when(way == side)
        def _():
            level = lax.broadcasted_iota(jnp.int32, (ents, edges), 0)
            put = jnp.where(level == ids_ref[pl.ds(row, 1), 0:edges], 1.0, 0.0).astype(BF)
            acc_ref[...] += jnp.dot(put, near_ref[j], preferred_element_type=F32)

        return carry

    lax.fori_loop(0, span_count(info_ref), span, 0)


def fold_kernel(stage, info_ref, got_ref, keep_ref, dep_ref, give_out, keep_out):
    bit = info_ref[stage]
    for i in range(give_out.shape[0]):
        give, stay = 2 * i + 1 - bit, 2 * i + bit
        give_out[i] = (got_ref[give].astype(F32) + keep_ref[give]).astype(BF)
        keep_out[i] = got_ref[stay].astype(F32) + keep_ref[stay]


def far_kernel(info_ref, acc_ref, got_ref, dep_ref, out_ref):
    @pl.when(info_ref[2] == 0)
    def _():
        out_ref[...] = (acc_ref[...] + got_ref[...]).astype(BF)


def grad_table_kernel(info_ref, acc_ref, near_ref, back_ref, dep_ref, out_ref):
    @pl.when(info_ref[2] == 0)
    def _():
        out_ref[...] = acc_ref[...] + near_ref[...]

    @pl.when(info_ref[2] != 0)
    def _():
        out_ref[...] = back_ref[...].astype(F32)


def grad_relation_kernel(*refs):
    out_ref, total = refs[-2:]
    pieces = out_ref.shape[1] // LANES
    part = out_ref.shape[0] // CHUNKS
    for h in range(CHUNKS):
        total[...] = refs[h][0].astype(F32) + refs[CHUNKS + h][0]
        for q in range(pieces):
            out_ref[h * part : (h + 1) * part, q * LANES : (q + 1) * LANES] = total[
                pl.ds(q, part, stride=pieces), :
            ]


def tie(x, dep):
    return pl.pallas_call(
        lambda x_ref, dep_ref, out_ref: None,
        out_shape=jax.ShapeDtypeStruct(x.shape, x.dtype),
        in_specs=[ANY, ANY],
        out_specs=ANY,
        input_output_aliases={0: 0},
        name="tie",
    )(x, dep)


def params(mib):
    return pltpu.CompilerParams(vmem_limit_bytes=mib << 20)


def shards(counts, src_index, dst_index, rel_index, neg_index, entity_table, relation_table):
    devices = lax.axis_size("ent")
    half = devices // 2
    cap, edges = src_index.shape
    ents, width = entity_table.shape
    rels = relation_table.shape[0]
    pieces = width // LANES
    shape = jax.ShapeDtypeStruct
    me = lax.axis_index("ent")
    leads = [i for i in range(half) if i % 2 == 0] + [i for i in range(half, devices) if i % 2 == 1]
    lead = (me % 2) == (me // half)

    cross = [((i + half) % devices, i) for i in leads]
    back = [(i, (i + half) % devices) for i in leads]
    to_mate = [(i, i ^ 1) for i in leads]
    from_mate = [(i ^ 1, i) for i in leads]

    step = -(-(cap + 1) // 8) * 8
    index_arrays = (src_index, dst_index, rel_index, neg_index)
    mine = pl.pallas_call(
        pack_kernel,
        out_shape=shape((step, sum(a.shape[1] for a in index_arrays)), jnp.int32),
        in_specs=[SMEM] + [ANY] * 4,
        out_specs=VMEM,
        scratch_shapes=[pltpu.VMEM(a.shape, jnp.int32) for a in index_arrays] + [pltpu.SemaphoreType.DMA((4,))],
        compiler_params=params(2),
        name="pack",
    )(counts, *index_arrays)
    cross_mate = [(a, b ^ 1) for a, b in cross]
    from_lead = lax.ppermute(mine, "ent", to_mate)
    first = jnp.where(lead, mine, from_lead)
    second = lax.ppermute(mine, "ent", cross) + lax.ppermute(mine, "ent", cross_mate)
    sent = pl.pallas_call(
        relay_kernel,
        out_shape=shape(entity_table.shape, BF),
        in_specs=[ANY, ANY],
        out_specs=VMEM,
        scratch_shapes=[pltpu.SemaphoreType.DMA],
        compiler_params=params(2),
        name="relay",
    )(entity_table, second)
    far = lax.ppermute(sent, "ent", cross)
    ids = jnp.concatenate([first[:cap], second[:cap]], axis=0)
    bits = [(me >> b) & 1 for b in range(devices.bit_length() - 1)]
    info = jnp.stack([first[cap, 0], second[cap, 0], jnp.where(lead, 0, 1), *bits]).astype(jnp.int32)
    ids_t = ids.T
    rel_ids = ids[:, 2 * edges : 3 * edges]

    rel_rows, mult = pl.pallas_call(
        functools.partial(prep_kernel, cap),
        out_shape=(shape((cap, edges, width), F32), shape((cap, 1, ents), F32)),
        in_specs=[SMEM, SMEM, VMEM, VMEM],
        out_specs=(VMEM, VMEM),
        compiler_params=params(8),
        cost_estimate=pl.CostEstimate(flops=1, bytes_accessed=1, transcendentals=0),
        name="prep",
    )(info, rel_ids, ids_t, relation_table)

    far = tie(far, mult)
    mate_table = lax.ppermute(entity_table, "ent", to_mate)
    mate_far = lax.ppermute(far, "ent", to_mate)

    block = (devices // 2, rels // devices // CHUNKS * pieces, LANES)
    mixed, scaled, near, *rest = pl.pallas_call(
        functools.partial(span_kernel, cap),
        out_shape=(
            shape((cap, edges, ents), BF),
            shape((cap, edges, width), BF),
            shape((cap, edges, width), BF),
            *[shape(block, F32)] * CHUNKS,
            *[shape(block, BF)] * CHUNKS,
        ),
        in_specs=[SMEM, SMEM, VMEM, VMEM, HBM, VMEM] + [ANY] * 4,
        out_specs=(VMEM,) * (3 + 2 * CHUNKS),
        scratch_shapes=[
            pltpu.VMEM((2, ents, width), BF),
            pltpu.VMEM((rels, pieces, LANES), F32),
            pltpu.VMEM((edges, pieces, LANES), F32),
            pltpu.VMEM((2, edges, width), F32),
            pltpu.SemaphoreType.DMA((2,)),
            pltpu.SemaphoreType.DMA((2,)),
        ],
        compiler_params=params(30),
        name="spans",
    )(info, rel_ids, ids_t, ids, rel_rows, mult, entity_table, far, mate_table, mate_far)
    keep, give = rest[:CHUNKS], rest[CHUNKS:]

    def table_side(side, dep):
        return pl.pallas_call(
            functools.partial(table_kernel, cap, side),
            out_shape=shape((ents, width), F32),
            in_specs=[SMEM] + [VMEM] * 4 + [ANY],
            out_specs=VMEM,
            compiler_params=params(8),
            cost_estimate=pl.CostEstimate(
                flops=2 * cap * edges * ents * width, bytes_accessed=12 << 20, transcendentals=0
            ),
            name="tables",
        )(info, ids, mixed, scaled, near, dep)

    far_acc = table_side(1, mixed)
    far_got = lax.ppermute(far_acc, "ent", from_mate)

    dep, near_acc, returned, bit = scaled, None, None, 1
    got = [lax.ppermute(g, "ent", [(i, i ^ bit) for i in range(devices)]) for g in give]
    while 2 * bit < devices:
        give = []
        for h in range(CHUNKS):
            half_block = (got[h].shape[0] // 2, *block[1:])
            g, keep[h] = pl.pallas_call(
                functools.partial(fold_kernel, 3 + bit.bit_length()),
                out_shape=(shape(half_block, BF), shape(half_block, F32)),
                in_specs=[SMEM, VMEM, VMEM, ANY],
                out_specs=(VMEM, VMEM),
                compiler_params=params(4),
                name="fold",
            )(info, got[h], keep[h], dep)
            dep = g
            give.append(g)
        if returned is None:
            far_sum = pl.pallas_call(
                far_kernel,
                out_shape=shape((ents, width), BF),
                in_specs=[SMEM, VMEM, VMEM, ANY],
                out_specs=VMEM,
                compiler_params=params(4),
                name="far_sum",
            )(info, far_acc, far_got, dep)
            returned = lax.ppermute(far_sum, "ent", back)
            dep = returned
        elif near_acc is None and 4 * bit >= devices:
            near_acc = table_side(0, give[0])
            near_got = lax.ppermute(near_acc, "ent", from_mate)
        bit *= 2
        got = [lax.ppermute(g, "ent", [(i, i ^ bit) for i in range(devices)]) for g in give]

    grad_table = pl.pallas_call(
        grad_table_kernel,
        out_shape=shape((ents, width), F32),
        in_specs=[SMEM, VMEM, VMEM, VMEM, ANY],
        out_specs=VMEM,
        compiler_params=params(4),
        name="grad_table",
    )(info, near_acc, near_got, returned, dep)
    grad_relation = pl.pallas_call(
        grad_relation_kernel,
        out_shape=shape((rels // devices, width), F32),
        in_specs=[VMEM] * (2 * CHUNKS),
        out_specs=VMEM,
        scratch_shapes=[pltpu.VMEM(block[1:], F32)],
        compiler_params=params(4),
        name="grad_relation",
    )(*got, *keep)
    return (grad_table, grad_relation)


def solution(mesh):
    in_specs = (
        P(("groups", "ent")),
        P(("groups", "ent"), None),
        P(("groups", "ent"), None),
        P(("groups", "ent"), None),
        P(("groups", "ent"), None),
        P(("groups", "ent"), None),
        P(),
    )
    out_specs = (P(("groups", "ent"), None), P(("groups", "ent"), None))
    return jax.shard_map(shards, mesh=mesh, in_specs=in_specs, out_specs=out_specs, check_vma=False)
```

```python
import functools

import jax
import jax.numpy as jnp
from jax import lax
from jax.experimental import pallas as pl
from jax.experimental.pallas import tpu as pltpu
from jax.sharding import PartitionSpec as P

margin = 0.1
BF = jnp.bfloat16
F32 = jnp.float32
BATCH = 16
LANES = 128
CHUNKS = 2

VMEM = pl.BlockSpec(memory_space=pltpu.VMEM)
SMEM = pl.BlockSpec(memory_space=pltpu.SMEM)
ANY = pl.BlockSpec(memory_space=pl.ANY)
HBM = pl.BlockSpec(memory_space=pltpu.HBM)


def list_row(info_ref, j, cap):
    pos = 2 * j + info_ref[2]
    second = pos >= info_ref[0]
    row = jnp.where(second, cap + pos - info_ref[0], pos)
    return row, second.astype(jnp.int32)


def span_count(info_ref):
    return (info_ref[0] + info_ref[1] + 1 - info_ref[2]) // 2


def pick_column(block, row):
    lane = lax.broadcasted_iota(jnp.int32, block.shape, 1)
    return jnp.sum(jnp.where(lane == row, block, 0), axis=1, keepdims=True)


def pack_kernel(counts_ref, *refs):
    arrays, out_ref, held, sems = refs[:4], refs[4], refs[5:9], refs[9]
    copies = [pltpu.make_async_copy(arrays[i], held[i], sems.at[i]) for i in range(4)]
    for copy in copies:
        copy.start()
    cap, length = arrays[0].shape[0], out_ref.shape[1]
    out_ref[...] = jnp.full(out_ref.shape, counts_ref[0], jnp.int32)
    at = 0
    for copy, ref in zip(copies, held):
        copy.wait()
        out_ref[:cap, at : at + ref.shape[1]] = ref[...]
        at += ref.shape[1]


def relay_kernel(x_ref, dep_ref, out_ref, sem):
    copy = pltpu.make_async_copy(x_ref, out_ref, sem)
    copy.start()
    copy.wait()


def prep_kernel(cap, info_ref, rel_ids_ref, ids_t_ref, table_ref, rows_ref, mult_ref):
    edges = rel_ids_ref.shape[1]
    ents = mult_ref.shape[2]

    def span(j, carry):
        row, _ = list_row(info_ref, j, cap)
        for e in range(edges):
            rows_ref[j, pl.ds(e, 1), :] = table_ref[pl.ds(rel_ids_ref[row, e], 1), :]
        total = jnp.zeros((8, ents), F32)
        neg = pick_column(ids_t_ref[3 * edges :, :], row)
        lane = lax.broadcasted_iota(jnp.int32, (8, ents), 1)
        for k in range(neg.shape[0] // 8):
            total = total + jnp.where(lane == neg[8 * k : 8 * k + 8], 1.0, 0.0)
        mult_ref[j] = jnp.sum(total, axis=0, keepdims=True)
        return carry

    lax.fori_loop(0, span_count(info_ref), span, 0)


def span_kernel(
    cap, info_ref, rel_ids_ref, ids_t_ref, ids_ref, rel_rows_ref, mult_ref,
    table_ref, far_ref, mate_table_ref, mate_far_ref,
    mixed_ref, scaled_ref, near_ref, *rest,
):
    keep_refs, give_refs = rest[:CHUNKS], rest[CHUNKS : 2 * CHUNKS]
    table, rel_acc, flat, rows, row_sems, table_sems = rest[2 * CHUNKS :]
    edges = rel_ids_ref.shape[1]
    ents = table_ref.shape[0]
    count = span_count(info_ref)

    @pl.when(info_ref[2] == 0)
    def _():
        pltpu.make_async_copy(table_ref, table.at[0], table_sems.at[0]).start()
        pltpu.make_async_copy(far_ref, table.at[1], table_sems.at[1]).start()

    @pl.when(info_ref[2] != 0)
    def _():
        pltpu.make_async_copy(mate_table_ref, table.at[0], table_sems.at[0]).start()
        pltpu.make_async_copy(mate_far_ref, table.at[1], table_sems.at[1]).start()

    def clear(i, c):
        rel_acc[pl.ds(i * 64, 64)] = jnp.zeros((64, *rel_acc.shape[1:]), F32)
        return c

    lax.fori_loop(0, rel_acc.shape[0] // 64, clear, 0)
    flat[...] = jnp.zeros(flat.shape, F32)
    pltpu.make_async_copy(table_ref, table.at[0], table_sems.at[0]).wait()
    pltpu.make_async_copy(far_ref, table.at[1], table_sems.at[1]).wait()

    def add_rows(row):
        for b in range(edges // BATCH):
            where_to = [rel_ids_ref[row, b * BATCH + i] for i in range(BATCH)]
            sums = [rel_acc[where_to[i]] + flat[b * BATCH + i] for i in range(BATCH)]
            for i in range(BATCH):
                rel_acc[where_to[i]] = sums[i]

    def fetch(j):
        slot = lax.rem(j, 2)
        return pltpu.make_async_copy(rel_rows_ref.at[j], rows.at[slot], row_sems.at[slot])

    @pl.when(count > 0)
    def _():
        fetch(0).start()

    e0 = lax.broadcasted_iota(jnp.int32, (edges, edges), 0) // BATCH
    e1 = lax.broadcasted_iota(jnp.int32, (edges, edges), 1) // BATCH

    def span(j, carry):
        fetch(j).wait()

        @pl.when(j + 1 < count)
        def _():
            fetch(j + 1).start()

        add_rows(list_row(info_ref, jnp.maximum(j - 1, 0), cap)[0])
        row, way = list_row(info_ref, j, cap)
        src = pick_column(ids_t_ref[0:edges, :], row)
        dst = pick_column(ids_t_ref[edges : 2 * edges, :], row)
        rel = pick_column(ids_t_ref[2 * edges : 3 * edges, :], row)
        rel_row = ids_ref[pl.ds(row, 1), 2 * edges : 3 * edges]
        lane = lax.broadcasted_iota(jnp.int32, (edges, ents), 1)
        far_table = table[1 - way]
        take = jnp.where(lane == src, 1.0, 0.0).astype(BF)
        source = jnp.dot(take, table[way], preferred_element_type=F32)
        rel_rows = rows[lax.rem(j, 2)]
        rotated = source * rel_rows
        score = lax.dot_general(
            rotated.astype(BF), far_table, (((1,), (1,)), ((), ())), preferred_element_type=F32
        )
        hit = lane == dst
        positive = jnp.sum(jnp.where(hit, score, 0.0), axis=1, keepdims=True)
        weights = mult_ref[j] / (1.0 + jnp.exp(positive - margin - score))
        totals = jnp.sum(weights, axis=1, keepdims=True)
        inverse = 1.0 / jnp.maximum(totals, 1e-30)
        mixed = (weights * inverse - jnp.where(hit, 1.0, 0.0)).astype(BF)
        mixed_ref[j] = mixed
        scaled_ref[j] = (rotated * totals).astype(BF)
        grad_rot = jnp.dot(mixed, far_table, preferred_element_type=F32) * totals
        near_ref[j] = (grad_rot * rel_rows).astype(BF)
        same = jnp.where((rel == rel_row) & (e0 == e1), 1.0, 0.0).astype(BF)
        grad_rel = grad_rot * source
        coarse = grad_rel.astype(BF)
        fine = (grad_rel - coarse.astype(F32)).astype(BF)
        summed = jnp.dot(same, coarse, preferred_element_type=F32) + jnp.dot(
            same, fine, preferred_element_type=F32
        )
        for q in range(flat.shape[1]):
            flat[:, q, :] = summed[:, q * LANES : (q + 1) * LANES]
        return carry

    lax.fori_loop(0, count, span, 0)

    @pl.when(count > 0)
    def _():
        add_rows(list_row(info_ref, jnp.maximum(count - 1, 0), cap)[0])

    pairs, part = keep_refs[0].shape[0], keep_refs[0].shape[1] // flat.shape[1]
    core = info_ref[3]

    def hand_out(c, carry):
        for h in range(CHUNKS):
            mine = (2 * c + core) * CHUNKS * part + h * part
            theirs = (2 * c + 1 - core) * CHUNKS * part + h * part
            keep_refs[h][c] = rel_acc[pl.ds(mine, part)].reshape(keep_refs[h].shape[1:])
            give_refs[h][c] = rel_acc[pl.ds(theirs, part)].reshape(keep_refs[h].shape[1:]).astype(BF)
        return carry

    lax.fori_loop(0, pairs, hand_out, 0)


def table_kernel(cap, side, info_ref, ids_ref, mixed_ref, scaled_ref, near_ref, dep_ref, acc_ref):
    edges, ents = near_ref.shape[1], acc_ref.shape[0]
    acc_ref[...] = jnp.zeros(acc_ref.shape, F32)

    def span(j, carry):
        row, way = list_row(info_ref, j, cap)

        @pl.when(way != side)
        def _():
            acc_ref[...] += lax.dot_general(
                mixed_ref[j], scaled_ref[j], (((0,), (0,)), ((), ())), preferred_element_type=F32
            )

        @pl.when(way == side)
        def _():
            level = lax.broadcasted_iota(jnp.int32, (ents, edges), 0)
            put = jnp.where(level == ids_ref[pl.ds(row, 1), 0:edges], 1.0, 0.0).astype(BF)
            acc_ref[...] += jnp.dot(put, near_ref[j], preferred_element_type=F32)

        return carry

    lax.fori_loop(0, span_count(info_ref), span, 0)


def fold_kernel(stage, info_ref, got_ref, keep_ref, dep_ref, give_out, keep_out):
    bit = info_ref[stage]
    for i in range(give_out.shape[0]):
        give, stay = 2 * i + 1 - bit, 2 * i + bit
        give_out[i] = (got_ref[give].astype(F32) + keep_ref[give]).astype(BF)
        keep_out[i] = got_ref[stay].astype(F32) + keep_ref[stay]


def far_kernel(info_ref, acc_ref, got_ref, dep_ref, out_ref):
    @pl.when(info_ref[2] == 0)
    def _():
        out_ref[...] = (acc_ref[...] + got_ref[...]).astype(BF)


def grad_table_kernel(info_ref, acc_ref, near_ref, back_ref, dep_ref, out_ref):
    @pl.when(info_ref[2] == 0)
    def _():
        out_ref[...] = acc_ref[...] + near_ref[...]

    @pl.when(info_ref[2] != 0)
    def _():
        out_ref[...] = back_ref[...].astype(F32)


def grad_relation_kernel(*refs):
    out_ref, total = refs[-2:]
    pieces = out_ref.shape[1] // LANES
    part = out_ref.shape[0] // CHUNKS
    for h in range(CHUNKS):
        total[...] = refs[h][0].astype(F32) + refs[CHUNKS + h][0]
        for q in range(pieces):
            out_ref[h * part : (h + 1) * part, q * LANES : (q + 1) * LANES] = total[
                pl.ds(q, part, stride=pieces), :
            ]


def tie(x, dep):
    return pl.pallas_call(
        lambda x_ref, dep_ref, out_ref: None,
        out_shape=jax.ShapeDtypeStruct(x.shape, x.dtype),
        in_specs=[ANY, ANY],
        out_specs=ANY,
        input_output_aliases={0: 0},
        name="tie",
    )(x, dep)


def params(mib):
    return pltpu.CompilerParams(vmem_limit_bytes=mib << 20)


def shards(counts, src_index, dst_index, rel_index, neg_index, entity_table, relation_table):
    devices = lax.axis_size("ent")
    half = devices // 2
    cap, edges = src_index.shape
    ents, width = entity_table.shape
    rels = relation_table.shape[0]
    pieces = width // LANES
    shape = jax.ShapeDtypeStruct
    me = lax.axis_index("ent")
    leads = [i for i in range(half) if i % 2 == 0] + [i for i in range(half, devices) if i % 2 == 1]
    lead = (me % 2) == (me // half)

    cross = [((i + half) % devices, i) for i in leads]
    back = [(i, (i + half) % devices) for i in leads]
    to_mate = [(i, i ^ 1) for i in leads]
    from_mate = [(i ^ 1, i) for i in leads]

    step = -(-(cap + 1) // 8) * 8
    index_arrays = (src_index, dst_index, rel_index, neg_index)
    mine = pl.pallas_call(
        pack_kernel,
        out_shape=shape((step, sum(a.shape[1] for a in index_arrays)), jnp.int32),
        in_specs=[SMEM] + [ANY] * 4,
        out_specs=VMEM,
        scratch_shapes=[pltpu.VMEM(a.shape, jnp.int32) for a in index_arrays] + [pltpu.SemaphoreType.DMA((4,))],
        compiler_params=params(2),
        name="pack",
    )(counts, *index_arrays)
    cross_mate = [(a, b ^ 1) for a, b in cross]
    from_lead = lax.ppermute(mine, "ent", to_mate)
    first = jnp.where(lead, mine, from_lead)
    second = lax.ppermute(mine, "ent", cross) + lax.ppermute(mine, "ent", cross_mate)
    sent = pl.pallas_call(
        relay_kernel,
        out_shape=shape(entity_table.shape, BF),
        in_specs=[ANY, ANY],
        out_specs=VMEM,
        scratch_shapes=[pltpu.SemaphoreType.DMA],
        compiler_params=params(2),
        name="relay",
    )(entity_table, second)
    far = lax.ppermute(sent, "ent", cross)
    ids = jnp.concatenate([first[:cap], second[:cap]], axis=0)
    bits = [(me >> b) & 1 for b in range(devices.bit_length() - 1)]
    info = jnp.stack([first[cap, 0], second[cap, 0], jnp.where(lead, 0, 1), *bits]).astype(jnp.int32)
    ids_t = ids.T
    rel_ids = ids[:, 2 * edges : 3 * edges]

    rel_rows, mult = pl.pallas_call(
        functools.partial(prep_kernel, cap),
        out_shape=(shape((cap, edges, width), F32), shape((cap, 1, ents), F32)),
        in_specs=[SMEM, SMEM, VMEM, VMEM],
        out_specs=(VMEM, VMEM),
        compiler_params=params(8),
        cost_estimate=pl.CostEstimate(flops=1, bytes_accessed=1, transcendentals=0),
        name="prep",
    )(info, rel_ids, ids_t, relation_table)

    far = tie(far, mult)
    mate_table = lax.ppermute(entity_table, "ent", to_mate)
    mate_far = lax.ppermute(far, "ent", to_mate)

    block = (devices // 2, rels // devices // CHUNKS * pieces, LANES)
    mixed, scaled, near, *rest = pl.pallas_call(
        functools.partial(span_kernel, cap),
        out_shape=(
            shape((cap, edges, ents), BF),
            shape((cap, edges, width), BF),
            shape((cap, edges, width), BF),
            *[shape(block, F32)] * CHUNKS,
            *[shape(block, BF)] * CHUNKS,
        ),
        in_specs=[SMEM, SMEM, VMEM, VMEM, HBM, VMEM] + [ANY] * 4,
        out_specs=(VMEM,) * (3 + 2 * CHUNKS),
        scratch_shapes=[
            pltpu.VMEM((2, ents, width), BF),
            pltpu.VMEM((rels, pieces, LANES), F32),
            pltpu.VMEM((edges, pieces, LANES), F32),
            pltpu.VMEM((2, edges, width), F32),
            pltpu.SemaphoreType.DMA((2,)),
            pltpu.SemaphoreType.DMA((2,)),
        ],
        compiler_params=params(30),
        name="spans",
    )(info, rel_ids, ids_t, ids, rel_rows, mult, entity_table, far, mate_table, mate_far)
    keep, give = rest[:CHUNKS], rest[CHUNKS:]

    def table_side(side, dep):
        return pl.pallas_call(
            functools.partial(table_kernel, cap, side),
            out_shape=shape((ents, width), F32),
            in_specs=[SMEM] + [VMEM] * 4 + [ANY],
            out_specs=VMEM,
            compiler_params=params(8),
            cost_estimate=pl.CostEstimate(
                flops=2 * cap * edges * ents * width, bytes_accessed=12 << 20, transcendentals=0
            ),
            name="tables",
        )(info, ids, mixed, scaled, near, dep)

    far_acc = table_side(1, mixed)
    far_got = lax.ppermute(far_acc, "ent", from_mate)

    near_acc = table_side(0, far_acc)
    near_got = lax.ppermute(near_acc, "ent", from_mate)

    dep, returned, bit = near_acc, None, 1
    got = [lax.ppermute(g, "ent", [(i, i ^ bit) for i in range(devices)]) for g in give]
    while 2 * bit < devices:
        give = []
        for h in range(CHUNKS):
            half_block = (got[h].shape[0] // 2, *block[1:])
            g, keep[h] = pl.pallas_call(
                functools.partial(fold_kernel, 3 + bit.bit_length()),
                out_shape=(shape(half_block, BF), shape(half_block, F32)),
                in_specs=[SMEM, VMEM, VMEM, ANY],
                out_specs=(VMEM, VMEM),
                compiler_params=params(4),
                name="fold",
            )(info, got[h], keep[h], dep)
            dep = g
            give.append(g)
        if returned is None:
            far_sum = pl.pallas_call(
                far_kernel,
                out_shape=shape((ents, width), BF),
                in_specs=[SMEM, VMEM, VMEM, ANY],
                out_specs=VMEM,
                compiler_params=params(4),
                name="far_sum",
            )(info, far_acc, far_got, dep)
            returned = lax.ppermute(far_sum, "ent", back)
            dep = returned
        bit *= 2
        got = [lax.ppermute(g, "ent", [(i, i ^ bit) for i in range(devices)]) for g in give]

    grad_table = pl.pallas_call(
        grad_table_kernel,
        out_shape=shape((ents, width), F32),
        in_specs=[SMEM, VMEM, VMEM, VMEM, ANY],
        out_specs=VMEM,
        compiler_params=params(4),
        name="grad_table",
    )(info, near_acc, near_got, returned, dep)
    grad_relation = pl.pallas_call(
        grad_relation_kernel,
        out_shape=shape((rels // devices, width), F32),
        in_specs=[VMEM] * (2 * CHUNKS),
        out_specs=VMEM,
        scratch_shapes=[pltpu.VMEM(block[1:], F32)],
        compiler_params=params(4),
        name="grad_relation",
    )(*got, *keep)
    return (grad_table, grad_relation)


def solution(mesh):
    in_specs = (
        P(("groups", "ent")),
        P(("groups", "ent"), None),
        P(("groups", "ent"), None),
        P(("groups", "ent"), None),
        P(("groups", "ent"), None),
        P(("groups", "ent"), None),
        P(),
    )
    out_specs = (P(("groups", "ent"), None), P(("groups", "ent"), None))
    return jax.shard_map(shards, mesh=mesh, in_specs=in_specs, out_specs=out_specs, check_vma=False)
```

```python
import functools

import jax
import jax.numpy as jnp
from jax import lax
from jax.experimental import pallas as pl
from jax.experimental.pallas import tpu as pltpu
from jax.sharding import PartitionSpec as P

margin = 0.1
BF = jnp.bfloat16
F32 = jnp.float32
BATCH = 16
LANES = 128
CHUNKS = 2

VMEM = pl.BlockSpec(memory_space=pltpu.VMEM)
SMEM = pl.BlockSpec(memory_space=pltpu.SMEM)
ANY = pl.BlockSpec(memory_space=pl.ANY)
HBM = pl.BlockSpec(memory_space=pltpu.HBM)


def list_row(info_ref, j, cap):
    pos = 2 * j + info_ref[2]
    second = pos >= info_ref[0]
    row = jnp.where(second, cap + pos - info_ref[0], pos)
    return row, second.astype(jnp.int32)


def span_count(info_ref):
    return (info_ref[0] + info_ref[1] + 1 - info_ref[2]) // 2


def pick_column(block, row):
    lane = lax.broadcasted_iota(jnp.int32, block.shape, 1)
    return jnp.sum(jnp.where(lane == row, block, 0), axis=1, keepdims=True)


def pack_kernel(counts_ref, *refs):
    arrays, out_ref, held, sems = refs[:4], refs[4], refs[5:9], refs[9]
    copies = [pltpu.make_async_copy(arrays[i], held[i], sems.at[i]) for i in range(4)]
    for copy in copies:
        copy.start()
    cap, length = arrays[0].shape[0], out_ref.shape[1]
    out_ref[...] = jnp.full(out_ref.shape, counts_ref[0], jnp.int32)
    at = 0
    for copy, ref in zip(copies, held):
        copy.wait()
        out_ref[:cap, at : at + ref.shape[1]] = ref[...]
        at += ref.shape[1]


def relay_kernel(x_ref, dep_ref, out_ref, sem):
    copy = pltpu.make_async_copy(x_ref, out_ref, sem)
    copy.start()
    copy.wait()


def prep_kernel(cap, info_ref, rel_ids_ref, ids_t_ref, table_ref, rows_ref, mult_ref):
    edges = rel_ids_ref.shape[1]
    ents = mult_ref.shape[2]

    def span(j, carry):
        row, _ = list_row(info_ref, j, cap)
        for e in range(edges):
            rows_ref[j, pl.ds(e, 1), :] = table_ref[pl.ds(rel_ids_ref[row, e], 1), :]
        total = jnp.zeros((8, ents), F32)
        neg = pick_column(ids_t_ref[3 * edges :, :], row)
        lane = lax.broadcasted_iota(jnp.int32, (8, ents), 1)
        for k in range(neg.shape[0] // 8):
            total = total + jnp.where(lane == neg[8 * k : 8 * k + 8], 1.0, 0.0)
        mult_ref[j] = jnp.sum(total, axis=0, keepdims=True)
        return carry

    lax.fori_loop(0, span_count(info_ref), span, 0)


def span_kernel(
    cap, info_ref, rel_ids_ref, ids_t_ref, ids_ref, rel_rows_ref, mult_ref,
    table_ref, far_ref, mate_table_ref, mate_far_ref,
    mixed_ref, scaled_ref, near_ref, *rest,
):
    keep_refs, give_refs = rest[:CHUNKS], rest[CHUNKS : 2 * CHUNKS]
    table, rel_acc, flat, rows, row_sems, table_sems = rest[2 * CHUNKS :]
    edges = rel_ids_ref.shape[1]
    ents = table_ref.shape[0]
    count = span_count(info_ref)

    @pl.when(info_ref[2] == 0)
    def _():
        pltpu.make_async_copy(table_ref, table.at[0], table_sems.at[0]).start()
        pltpu.make_async_copy(far_ref, table.at[1], table_sems.at[1]).start()

    @pl.when(info_ref[2] != 0)
    def _():
        pltpu.make_async_copy(mate_table_ref, table.at[0], table_sems.at[0]).start()
        pltpu.make_async_copy(mate_far_ref, table.at[1], table_sems.at[1]).start()

    def clear(i, c):
        rel_acc[pl.ds(i * 64, 64)] = jnp.zeros((64, *rel_acc.shape[1:]), F32)
        return c

    lax.fori_loop(0, rel_acc.shape[0] // 64, clear, 0)
    flat[...] = jnp.zeros(flat.shape, F32)
    pltpu.make_async_copy(table_ref, table.at[0], table_sems.at[0]).wait()
    pltpu.make_async_copy(far_ref, table.at[1], table_sems.at[1]).wait()

    def add_rows(row):
        for b in range(edges // BATCH):
            where_to = [rel_ids_ref[row, b * BATCH + i] for i in range(BATCH)]
            sums = [rel_acc[where_to[i]] + flat[b * BATCH + i] for i in range(BATCH)]
            for i in range(BATCH):
                rel_acc[where_to[i]] = sums[i]

    def fetch(j):
        slot = lax.rem(j, 2)
        return pltpu.make_async_copy(rel_rows_ref.at[j], rows.at[slot], row_sems.at[slot])

    @pl.when(count > 0)
    def _():
        fetch(0).start()

    e0 = lax.broadcasted_iota(jnp.int32, (edges, edges), 0) // BATCH
    e1 = lax.broadcasted_iota(jnp.int32, (edges, edges), 1) // BATCH

    def span(j, carry):
        fetch(j).wait()

        @pl.when(j + 1 < count)
        def _():
            fetch(j + 1).start()

        add_rows(list_row(info_ref, jnp.maximum(j - 1, 0), cap)[0])
        row, way = list_row(info_ref, j, cap)
        src = pick_column(ids_t_ref[0:edges, :], row)
        dst = pick_column(ids_t_ref[edges : 2 * edges, :], row)
        rel = pick_column(ids_t_ref[2 * edges : 3 * edges, :], row)
        rel_row = ids_ref[pl.ds(row, 1), 2 * edges : 3 * edges]
        lane = lax.broadcasted_iota(jnp.int32, (edges, ents), 1)
        far_table = table[1 - way]
        take = jnp.where(lane == src, 1.0, 0.0).astype(BF)
        source = jnp.dot(take, table[way], preferred_element_type=F32)
        rel_rows = rows[lax.rem(j, 2)]
        rotated = source * rel_rows
        score = lax.dot_general(
            rotated.astype(BF), far_table, (((1,), (1,)), ((), ())), preferred_element_type=F32
        )
        hit = lane == dst
        positive = jnp.sum(jnp.where(hit, score, 0.0), axis=1, keepdims=True)
        weights = mult_ref[j] / (1.0 + jnp.exp(positive - margin - score))
        totals = jnp.sum(weights, axis=1, keepdims=True)
        inverse = 1.0 / jnp.maximum(totals, 1e-30)
        mixed = (weights * inverse - jnp.where(hit, 1.0, 0.0)).astype(BF)
        mixed_ref[j] = mixed
        scaled_ref[j] = (rotated * totals).astype(BF)
        grad_rot = jnp.dot(mixed, far_table, preferred_element_type=F32) * totals
        near_ref[j] = (grad_rot * rel_rows).astype(BF)
        same = jnp.where((rel == rel_row) & (e0 == e1), 1.0, 0.0).astype(BF)
        grad_rel = grad_rot * source
        coarse = grad_rel.astype(BF)
        fine = (grad_rel - coarse.astype(F32)).astype(BF)
        summed = jnp.dot(same, coarse, preferred_element_type=F32) + jnp.dot(
            same, fine, preferred_element_type=F32
        )
        for q in range(flat.shape[1]):
            flat[:, q, :] = summed[:, q * LANES : (q + 1) * LANES]
        return carry

    lax.fori_loop(0, count, span, 0)

    @pl.when(count > 0)
    def _():
        add_rows(list_row(info_ref, jnp.maximum(count - 1, 0), cap)[0])

    pairs, part = keep_refs[0].shape[0], keep_refs[0].shape[1] // flat.shape[1]
    core = info_ref[3]

    def hand_out(c, carry):
        for h in range(CHUNKS):
            mine = (2 * c + core) * CHUNKS * part + h * part
            theirs = (2 * c + 1 - core) * CHUNKS * part + h * part
            keep_refs[h][c] = rel_acc[pl.ds(mine, part)].reshape(keep_refs[h].shape[1:])
            give_refs[h][c] = rel_acc[pl.ds(theirs, part)].reshape(keep_refs[h].shape[1:]).astype(BF)
        return carry

    lax.fori_loop(0, pairs, hand_out, 0)


def table_kernel(cap, side, info_ref, ids_ref, mixed_ref, scaled_ref, near_ref, dep_ref, acc_ref):
    edges, ents = near_ref.shape[1], acc_ref.shape[0]
    acc_ref[...] = jnp.zeros(acc_ref.shape, F32)

    def span(j, carry):
        row, way = list_row(info_ref, j, cap)

        @pl.when(way != side)
        def _():
            acc_ref[...] += lax.dot_general(
                mixed_ref[j], scaled_ref[j], (((0,), (0,)), ((), ())), preferred_element_type=F32
            )

        @pl.when(way == side)
        def _():
            level = lax.broadcasted_iota(jnp.int32, (ents, edges), 0)
            put = jnp.where(level == ids_ref[pl.ds(row, 1), 0:edges], 1.0, 0.0).astype(BF)
            acc_ref[...] += jnp.dot(put, near_ref[j], preferred_element_type=F32)

        return carry

    lax.fori_loop(0, span_count(info_ref), span, 0)


def fold_kernel(stage, info_ref, got_ref, keep_ref, dep_ref, give_out, keep_out):
    bit = info_ref[stage]
    for i in range(give_out.shape[0]):
        give, stay = 2 * i + 1 - bit, 2 * i + bit
        give_out[i] = (got_ref[give].astype(F32) + keep_ref[give]).astype(BF)
        keep_out[i] = got_ref[stay].astype(F32) + keep_ref[stay]


def far_kernel(info_ref, acc_ref, got_ref, dep_ref, out_ref):
    @pl.when(info_ref[2] == 0)
    def _():
        out_ref[...] = (acc_ref[...] + got_ref[...]).astype(BF)


def grad_table_kernel(info_ref, acc_ref, near_ref, back_ref, dep_ref, out_ref):
    @pl.when(info_ref[2] == 0)
    def _():
        out_ref[...] = acc_ref[...] + near_ref[...]

    @pl.when(info_ref[2] != 0)
    def _():
        out_ref[...] = back_ref[...].astype(F32)


def grad_relation_kernel(*refs):
    out_ref, total = refs[-2:]
    pieces = out_ref.shape[1] // LANES
    part = out_ref.shape[0] // CHUNKS
    for h in range(CHUNKS):
        total[...] = refs[h][0].astype(F32) + refs[CHUNKS + h][0]
        for q in range(pieces):
            out_ref[h * part : (h + 1) * part, q * LANES : (q + 1) * LANES] = total[
                pl.ds(q, part, stride=pieces), :
            ]


def relay(x, dep):
    return pl.pallas_call(
        relay_kernel,
        out_shape=jax.ShapeDtypeStruct(x.shape, x.dtype),
        in_specs=[ANY, ANY],
        out_specs=VMEM,
        scratch_shapes=[pltpu.SemaphoreType.DMA],
        compiler_params=params(2),
        name="relay",
    )(x, dep)


def params(mib):
    return pltpu.CompilerParams(vmem_limit_bytes=mib << 20)


def shards(counts, src_index, dst_index, rel_index, neg_index, entity_table, relation_table):
    devices = lax.axis_size("ent")
    half = devices // 2
    cap, edges = src_index.shape
    ents, width = entity_table.shape
    rels = relation_table.shape[0]
    pieces = width // LANES
    shape = jax.ShapeDtypeStruct
    me = lax.axis_index("ent")
    leads = [i for i in range(half) if i % 2 == 0] + [i for i in range(half, devices) if i % 2 == 1]
    lead = (me % 2) == (me // half)

    cross = [((i + half) % devices, i) for i in leads]
    back = [(i, (i + half) % devices) for i in leads]
    to_mate = [(i, i ^ 1) for i in leads]
    from_mate = [(i ^ 1, i) for i in leads]

    step = -(-(cap + 1) // 8) * 8
    index_arrays = (src_index, dst_index, rel_index, neg_index)
    mine = pl.pallas_call(
        pack_kernel,
        out_shape=shape((step, sum(a.shape[1] for a in index_arrays)), jnp.int32),
        in_specs=[SMEM] + [ANY] * 4,
        out_specs=VMEM,
        scratch_shapes=[pltpu.VMEM(a.shape, jnp.int32) for a in index_arrays] + [pltpu.SemaphoreType.DMA((4,))],
        compiler_params=params(2),
        name="pack",
    )(counts, *index_arrays)
    cross_mate = [(a, b ^ 1) for a, b in cross]
    from_lead = lax.ppermute(mine, "ent", to_mate)
    first = jnp.where(lead, mine, from_lead)
    second = lax.ppermute(mine, "ent", cross) + lax.ppermute(mine, "ent", cross_mate)
    sent = relay(entity_table, second)
    far = lax.ppermute(sent, "ent", cross)
    ids = jnp.concatenate([first[:cap], second[:cap]], axis=0)
    bits = [(me >> b) & 1 for b in range(devices.bit_length() - 1)]
    info = jnp.stack([first[cap, 0], second[cap, 0], jnp.where(lead, 0, 1), *bits]).astype(jnp.int32)
    ids_t = ids.T
    rel_ids = ids[:, 2 * edges : 3 * edges]

    rel_rows, mult = pl.pallas_call(
        functools.partial(prep_kernel, cap),
        out_shape=(shape((cap, edges, width), F32), shape((cap, 1, ents), F32)),
        in_specs=[SMEM, SMEM, VMEM, VMEM],
        out_specs=(VMEM, VMEM),
        compiler_params=params(8),
        cost_estimate=pl.CostEstimate(flops=1, bytes_accessed=1, transcendentals=0),
        name="prep",
    )(info, rel_ids, ids_t, relation_table)

    far = relay(far, rel_rows)
    mate_table = lax.ppermute(entity_table, "ent", to_mate)
    mate_far = lax.ppermute(far, "ent", to_mate)

    block = (devices // 2, rels // devices // CHUNKS * pieces, LANES)
    mixed, scaled, near, *rest = pl.pallas_call(
        functools.partial(span_kernel, cap),
        out_shape=(
            shape((cap, edges, ents), BF),
            shape((cap, edges, width), BF),
            shape((cap, edges, width), BF),
            *[shape(block, F32)] * CHUNKS,
            *[shape(block, BF)] * CHUNKS,
        ),
        in_specs=[SMEM, SMEM, VMEM, VMEM, HBM, VMEM] + [ANY] * 4,
        out_specs=(VMEM,) * (3 + 2 * CHUNKS),
        scratch_shapes=[
            pltpu.VMEM((2, ents, width), BF),
            pltpu.VMEM((rels, pieces, LANES), F32),
            pltpu.VMEM((edges, pieces, LANES), F32),
            pltpu.VMEM((2, edges, width), F32),
            pltpu.SemaphoreType.DMA((2,)),
            pltpu.SemaphoreType.DMA((2,)),
        ],
        compiler_params=params(30),
        name="spans",
    )(info, rel_ids, ids_t, ids, rel_rows, mult, entity_table, far, mate_table, mate_far)
    keep, give = rest[:CHUNKS], rest[CHUNKS:]

    def table_side(side, dep):
        return pl.pallas_call(
            functools.partial(table_kernel, cap, side),
            out_shape=shape((ents, width), F32),
            in_specs=[SMEM] + [VMEM] * 4 + [ANY],
            out_specs=VMEM,
            compiler_params=params(8),
            cost_estimate=pl.CostEstimate(
                flops=2 * cap * edges * ents * width, bytes_accessed=12 << 20, transcendentals=0
            ),
            name="tables",
        )(info, ids, mixed, scaled, near, dep)

    far_acc = table_side(1, mixed)
    far_got = lax.ppermute(far_acc, "ent", from_mate)

    near_acc = table_side(0, far_acc)
    near_got = lax.ppermute(near_acc, "ent", from_mate)

    dep, returned, bit = near_acc, None, 1
    got = [lax.ppermute(g, "ent", [(i, i ^ bit) for i in range(devices)]) for g in give]
    while 2 * bit < devices:
        give = []
        for h in range(CHUNKS):
            half_block = (got[h].shape[0] // 2, *block[1:])
            g, keep[h] = pl.pallas_call(
                functools.partial(fold_kernel, 3 + bit.bit_length()),
                out_shape=(shape(half_block, BF), shape(half_block, F32)),
                in_specs=[SMEM, VMEM, VMEM, ANY],
                out_specs=(VMEM, VMEM),
                compiler_params=params(4),
                name="fold",
            )(info, got[h], keep[h], dep)
            dep = g
            give.append(g)
        if returned is None:
            far_sum = pl.pallas_call(
                far_kernel,
                out_shape=shape((ents, width), BF),
                in_specs=[SMEM, VMEM, VMEM, ANY],
                out_specs=VMEM,
                compiler_params=params(4),
                name="far_sum",
            )(info, far_acc, far_got, dep)
            returned = lax.ppermute(far_sum, "ent", back)
            dep = returned
        bit *= 2
        got = [lax.ppermute(g, "ent", [(i, i ^ bit) for i in range(devices)]) for g in give]

    grad_table = pl.pallas_call(
        grad_table_kernel,
        out_shape=shape((ents, width), F32),
        in_specs=[SMEM, VMEM, VMEM, VMEM, ANY],
        out_specs=VMEM,
        compiler_params=params(4),
        name="grad_table",
    )(info, near_acc, near_got, returned, dep)
    grad_relation = pl.pallas_call(
        grad_relation_kernel,
        out_shape=shape((rels // devices, width), F32),
        in_specs=[VMEM] * (2 * CHUNKS),
        out_specs=VMEM,
        scratch_shapes=[pltpu.VMEM(block[1:], F32)],
        compiler_params=params(4),
        name="grad_relation",
    )(*got, *keep)
    return (grad_table, grad_relation)


def solution(mesh):
    in_specs = (
        P(("groups", "ent")),
        P(("groups", "ent"), None),
        P(("groups", "ent"), None),
        P(("groups", "ent"), None),
        P(("groups", "ent"), None),
        P(("groups", "ent"), None),
        P(),
    )
    out_specs = (P(("groups", "ent"), None), P(("groups", "ent"), None))
    return jax.shard_map(shards, mesh=mesh, in_specs=in_specs, out_specs=out_specs, check_vma=False)
```
